32 devices in a mesh: groups: 2 (over x), wide: 8 (over z, y), narrow: 2 (over core).
Axes of the slice: x: 2, y: 2, z: 4, core: 2. Of those that a mesh axis runs over, the one named last changes fastest.
Arguments:
- draft_rows: bfloat16 [256, 8192], P(('groups', 'wide'), 'narrow'), parts along dimension 0, may hold values from -6 to 6
- gate_weight: bfloat16 [8192, 4096], P('narrow', 'wide'), may hold values from -0.0625 to 0.0625
- up_weight: bfloat16 [8192, 4096], P('narrow', 'wide'), may hold values from -0.0625 to 0.0625
- down_weight: bfloat16 [4096, 8192], P('wide', 'narrow'), may hold values from -0.09375 to 0.09375
Outputs:
- ffn_out: bfloat16 [256, 8192], P(('groups', 'wide'), 'narrow'), parts along dimension 0
The draws below stay inside these ranges and needn't reach their ends.
There are 2 independent parts, one for each index of `groups`. The reference program is written for one: setup_inputs(seed, part) draws one part's arguments, and reference() takes and returns one part's arrays. A program takes and returns all parts, laid end to end along the dimension named above; an argument that names none is the same for every part. Nothing has to cross between parts.
All inputs are finite; a program needn't handle non-finite values.
Results may differ from the reference program's by a relative error of at most 0.0049.
Values may be sent and summed in bfloat16 or wider, within the bound.
A program may use at most 64 MiB of HBM per device.

```python
import jax
import jax.numpy as jnp

D = 8192
FF = 4096
ROWS = 128


def levels(stream_key, extent, cuts, least, high):
    def one(dim, blocks):
        draws = jax.random.uniform(jax.random.fold_in(jax.random.fold_in(stream_key, 6), dim), (blocks,), jnp.float32, least / len(cuts), high / len(cuts))
        return jnp.repeat(jnp.exp(draws), extent[dim] // blocks).reshape((-1,) + (1,) * (len(extent) - dim - 1))

    loudness = one(*cuts[0])
    for cut in cuts[1:]:
        loudness = loudness * one(*cut)
    return loudness


def scatter_about(stream_key, shape, deviation, bound, cuts=(), held_as=jnp.bfloat16):
    entries = jax.random.normal(stream_key, shape, jnp.float32) * deviation
    if len(cuts) > 0:
        entries = levels(stream_key, shape, cuts, -0.22, 0.18) * entries
    return jnp.clip(entries, min=-bound, max=bound).astype(held_as)


def setup_inputs(seed: int = 0, part: int = 0) -> dict:
    key_of = jax.random.split(jax.random.key(seed), 5)
    part_keys = jax.random.split(jax.random.fold_in(key_of[4], part), 5)
    return {
        "draft_rows": scatter_about(part_keys[0], (ROWS, D), 1.0, 6.0, ((0, 8), (1, 2))),
        "gate_weight": scatter_about(key_of[1], (D, FF), D ** -0.5, 0.0625, ((0, 2), (1, 8))),
        "up_weight": scatter_about(key_of[2], (D, FF), D ** -0.5, 0.0625, ((0, 2), (1, 8))),
        "down_weight": scatter_about(key_of[3], (FF, D), FF ** -0.5, 0.09375, ((0, 8), (1, 2))),
    }


def reference(draft_rows, gate_weight, up_weight, down_weight):
    gate_sum = jnp.dot(draft_rows, gate_weight, preferred_element_type=jnp.float32)
    up_sum = jnp.dot(draft_rows, up_weight, preferred_element_type=jnp.float32)
    hidden = (jax.nn.silu(gate_sum) * up_sum).astype(jnp.bfloat16)
    return jnp.dot(hidden, down_weight, preferred_element_type=jnp.float32).astype(jnp.bfloat16)
```

```python
import functools

import jax
import jax.numpy as jnp
from jax import lax
from jax.experimental import pallas as pl
from jax.experimental.pallas import tpu as pltpu
from jax.sharding import PartitionSpec as P

MESH = pl.DeviceIdType.MESH
COLUMN = 2
DEPTH_CHUNKS = 4
HIDDEN_TILES = 2
OUT_CHUNKS = 8


def kernel(wide, x_hbm, gate_hbm, up_hbm, down_hbm, out_ref,
           xg, gate, up, down, acc, peer, hid, own, y_out, y_in, z_out, z_in,
           w_sem, d_sem, x_sem, zs, zr, ys, yr, ns, nr, rys, ryr, rzs, rzr):
    zn = wide // COLUMN
    rows, width = x_hbm.shape
    half = zn * rows
    units = gate_hbm.shape[1]
    depth = width // DEPTH_CHUNKS
    tile = units // HIDDEN_TILES
    cols = width // OUT_CHUNKS

    me = lax.axis_index("wide")
    z, y = me // COLUMN, lax.rem(me, COLUMN)
    core = lax.axis_index("narrow")
    across = {"wide": z * COLUMN + (1 - y)}
    twin = {"narrow": 1 - core}

    def along(d):
        return {"wide": lax.rem(z + d, zn) * COLUMN + y}

    def local(k):
        part = pl.ds(k * depth, depth)
        return [
            pltpu.make_async_copy(gate_hbm.at[part], gate.at[part], w_sem.at[0, k]),
            pltpu.make_async_copy(up_hbm.at[part], up.at[part], w_sem.at[1, k]),
        ]

    def remote(src, dst, send, recv, to):
        return pltpu.make_async_remote_copy(
            src_ref=src, dst_ref=dst, send_sem=send, recv_sem=recv, device_id=to, device_id_type=MESH)

    mine = pltpu.make_async_copy(x_hbm, xg.at[0], x_sem)
    mine.start()
    for k in range(DEPTH_CHUNKS):
        for copy in local(k):
            copy.start()
    down_copy = pltpu.make_async_copy(down_hbm, down, d_sem)
    down_copy.start()

    barrier = pltpu.get_barrier_semaphore()
    for d in range(1, zn):
        pl.semaphore_signal(barrier, inc=1, device_id=along(d), device_id_type=MESH)
    pl.semaphore_signal(barrier, inc=1, device_id=across, device_id_type=MESH)
    pl.semaphore_signal(barrier, inc=1, device_id=twin, device_id_type=MESH)
    pl.semaphore_wait(barrier, zn + 1)

    def z_copy(k, d):
        part = pl.ds(k * depth, depth)
        return remote(x_hbm.at[:, part], xg.at[zn - d, :, part], zs.at[k, d], zr.at[k, zn - d], along(d))

    def y_copy(k, s):
        part = pl.ds(k * depth, depth)
        src = x_hbm.at[:, part] if s == 0 else xg.at[s, :, part]
        return remote(src, xg.at[zn + s, :, part], ys.at[k, s], yr.at[k, s], across)

    for k in range(DEPTH_CHUNKS):
        y_copy(k, 0).start()
        for d in range(1, zn):
            z_copy(k, d).start()

    def relay(k):
        for s in sorted(range(1, zn), key=lambda s: min(s, zn - s)):
            z_copy(k, zn - s).wait_recv()
            y_copy(k, s).start()

    def twin_copy(t):
        return remote(acc.at[t], peer.at[t], ns.at[t], nr.at[t], twin)

    def project(k):
        for s in range(zn):
            y_copy(k, s).wait_recv()
        for copy in local(k):
            copy.wait()
        part = pl.ds(k * depth, depth)
        x = xg[:, :, part].reshape(2 * half, depth)
        for t in range(HIDDEN_TILES):
            mid = pl.ds(t * tile, tile)
            for i, weight in enumerate((gate, up)):
                value = jnp.dot(x, weight[part, mid], preferred_element_type=jnp.float32)
                place = pl.ds(i * tile, tile)
                if k == 0:
                    acc[t, :, place] = value
                else:
                    acc[t, :, place] += value
            if k == DEPTH_CHUNKS - 1:
                twin_copy(t).start()

    mine.wait()
    for k in range(DEPTH_CHUNKS):
        relay(k)
        if k > 0:
            project(k - 1)
    project(DEPTH_CHUNKS - 1)

    for t in range(HIDDEN_TILES):
        twin_copy(t).wait_recv()
        total = acc[t] + peer[t]
        gate_sum, up_sum = total[:, :tile], total[:, tile:]
        hid[:, pl.ds(t * tile, tile)] = (gate_sum / (1 + jnp.exp(-gate_sum)) * up_sum).astype(jnp.bfloat16)

    down_copy.wait()

    def ry_copy(n):
        return remote(y_out.at[n], y_in.at[n], rys.at[n], ryr.at[n], across)

    def rz_copy(n, d):
        return remote(z_out.at[n, d], z_in.at[n, zn - d], rzs.at[n, d], rzr.at[n, zn - d], along(d))

    for n in range(OUT_CHUNKS):
        products = jnp.dot(hid[...], down[:, pl.ds(n * cols, cols)], preferred_element_type=jnp.float32)
        y_out[n] = products[half:].astype(jnp.bfloat16)
        ry_copy(n).start()
        own[n] = products[:half]

    for n in range(OUT_CHUNKS):
        ry_copy(n).wait_recv()
        for d in range(zn):
            row = pl.ds(d * rows, rows)
            value = own[n, row] + y_in[n, row].astype(jnp.float32)
            if d == 0:
                own[n, row] = value
            else:
                z_out[n, d] = value.astype(jnp.bfloat16)
                rz_copy(n, d).start()

    for n in range(OUT_CHUNKS):
        value = own[n, pl.ds(0, rows)]
        for s in range(1, zn):
            rz_copy(n, zn - s).wait_recv()
            value = value + z_in[n, s].astype(jnp.float32)
        out_ref[:, pl.ds(n * cols, cols)] = value.astype(jnp.bfloat16)

    for k in range(DEPTH_CHUNKS):
        for d in range(zn):
            y_copy(k, d).wait_send()
            if d > 0:
                z_copy(k, d).wait_send()
    for t in range(HIDDEN_TILES):
        twin_copy(t).wait_send()
    for n in range(OUT_CHUNKS):
        ry_copy(n).wait_send()
        for d in range(1, zn):
            rz_copy(n, d).wait_send()


def solution(mesh):
    wide = mesh.shape["wide"]
    zn = wide // COLUMN

    def body(x, gate, up, down):
        rows, width = x.shape
        units = gate.shape[1]
        half, cols, tile = zn * rows, width // OUT_CHUNKS, units // HIDDEN_TILES
        bf16, f32 = jnp.bfloat16, jnp.float32
        dma = pltpu.SemaphoreType.DMA
        return pl.pallas_call(
            functools.partial(kernel, wide),
            out_shape=jax.ShapeDtypeStruct((rows, width), bf16),
            in_specs=[pl.BlockSpec(memory_space=pltpu.HBM)] * 4,
            out_specs=pl.BlockSpec(memory_space=pltpu.VMEM),
            scratch_shapes=[
                pltpu.VMEM((wide, rows, width), bf16),
                pltpu.VMEM(gate.shape, bf16),
                pltpu.VMEM(up.shape, bf16),
                pltpu.VMEM(down.shape, bf16),
                pltpu.VMEM((HIDDEN_TILES, 2 * half, 2 * tile), f32),
                pltpu.VMEM((HIDDEN_TILES, 2 * half, 2 * tile), f32),
                pltpu.VMEM((2 * half, units), bf16),
                pltpu.VMEM((OUT_CHUNKS, half, cols), f32),
                pltpu.VMEM((OUT_CHUNKS, half, cols), bf16),
                pltpu.VMEM((OUT_CHUNKS, half, cols), bf16),
                pltpu.VMEM((OUT_CHUNKS, zn, rows, cols), bf16),
                pltpu.VMEM((OUT_CHUNKS, zn, rows, cols), bf16),
                dma((2, DEPTH_CHUNKS)), dma, dma,
                dma((DEPTH_CHUNKS, zn)), dma((DEPTH_CHUNKS, zn)),
                dma((DEPTH_CHUNKS, zn)), dma((DEPTH_CHUNKS, zn)),
                dma((HIDDEN_TILES,)), dma((HIDDEN_TILES,)),
                dma((OUT_CHUNKS,)), dma((OUT_CHUNKS,)),
                dma((OUT_CHUNKS, zn)), dma((OUT_CHUNKS, zn)),
            ],
            compiler_params=pltpu.CompilerParams(
                collective_id=0, has_side_effects=True, vmem_limit_bytes=56 * 1024 * 1024),
        )(x, gate, up, down)

    in_specs = (
        P(("groups", "wide"), "narrow"),
        P("narrow", "wide"),
        P("narrow", "wide"),
        P("wide", "narrow"),
    )
    out_specs = P(("groups", "wide"), "narrow")
    return jax.shard_map(body, mesh=mesh, in_specs=in_specs, out_specs=out_specs, check_vma=False)
```

```python
import functools

import jax
import jax.numpy as jnp
from jax import lax
from jax.experimental import pallas as pl
from jax.experimental.pallas import tpu as pltpu
from jax.sharding import PartitionSpec as P

MESH = pl.DeviceIdType.MESH
COLUMN = 2
DEPTH_PARTS = (1, 2, 1)
DEPTH_CHUNKS = len(DEPTH_PARTS)
HIDDEN_TILES = 1
OUT_CHUNKS = 8
Z_FIRST = 2


def kernel(wide, x_hbm, gate_hbm, up_hbm, down_hbm, out_ref,
           xg, gate, up, down, acc, peer, hid, own, y_out, y_in, z_out, z_in, b_out, b_in, e_out, e_in,
           w_sem, d_sem, x_sem, zs, zr, ys, yr, ns, nr, rys, ryr, rzs, rzr,
           rbs, rbr, res, rer):
    zn = wide // COLUMN
    rows, width = x_hbm.shape
    half = zn * rows
    units = gate_hbm.shape[1]
    unit = width // sum(DEPTH_PARTS)
    tile = units // HIDDEN_TILES
    cols = width // OUT_CHUNKS

    me = lax.axis_index("wide")
    z, y = me // COLUMN, lax.rem(me, COLUMN)
    core = lax.axis_index("narrow")
    across = {"wide": z * COLUMN + (1 - y)}
    twin = {"narrow": 1 - core}

    def along(d):
        return {"wide": lax.rem(z + d, zn) * COLUMN + y}

    def span(k):
        return pl.ds(sum(DEPTH_PARTS[:k]) * unit, DEPTH_PARTS[k] * unit)

    def local(k):
        part = span(k)
        return [
            pltpu.make_async_copy(gate_hbm.at[part], gate.at[part], w_sem.at[0, k]),
            pltpu.make_async_copy(up_hbm.at[part], up.at[part], w_sem.at[1, k]),
        ]

    def remote(src, dst, send, recv, to):
        return pltpu.make_async_remote_copy(
            src_ref=src, dst_ref=dst, send_sem=send, recv_sem=recv, device_id=to, device_id_type=MESH)

    mine = pltpu.make_async_copy(x_hbm, xg.at[0], x_sem)
    mine.start()
    for k in range(DEPTH_CHUNKS):
        for copy in local(k):
            copy.start()
    down_copy = pltpu.make_async_copy(down_hbm, down, d_sem)
    down_copy.start()

    barrier = pltpu.get_barrier_semaphore()
    for d in range(1, zn):
        pl.semaphore_signal(barrier, inc=1, device_id=along(d), device_id_type=MESH)
    pl.semaphore_signal(barrier, inc=1, device_id=across, device_id_type=MESH)
    pl.semaphore_signal(barrier, inc=1, device_id=twin, device_id_type=MESH)
    pl.semaphore_wait(barrier, zn + 1)

    def z_copy(k, d):
        part = span(k)
        return remote(x_hbm.at[:, part], xg.at[zn - d, :, part], zs.at[k, d], zr.at[k, zn - d], along(d))

    def y_copy(k, s):
        part = span(k)
        src = x_hbm.at[:, part] if s == 0 else xg.at[s, :, part]
        return remote(src, xg.at[zn + s, :, part], ys.at[k, s], yr.at[k, s], across)

    for k in range(DEPTH_CHUNKS):
        y_copy(k, 0).start()
        for d in range(1, zn):
            z_copy(k, d).start()

    def relay(k):
        for s in sorted(range(1, zn), key=lambda s: min(s, zn - s)):
            z_copy(k, zn - s).wait_recv()
            y_copy(k, s).start()

    def twin_copy(t):
        return remote(acc.at[t], peer.at[t], ns.at[t], nr.at[t], twin)

    def project(k):
        for s in range(zn):
            y_copy(k, s).wait_recv()
        for copy in local(k):
            copy.wait()
        part = span(k)
        x = xg[:, :, part].reshape(2 * half, DEPTH_PARTS[k] * unit)
        for t in range(HIDDEN_TILES):
            mid = pl.ds(t * tile, tile)
            for i, weight in enumerate((gate, up)):
                value = jnp.dot(x, weight[part, mid], preferred_element_type=jnp.float32)
                place = pl.ds(i * tile, tile)
                if k == 0:
                    acc[t, :, place] = value
                else:
                    acc[t, :, place] += value
            if k == DEPTH_CHUNKS - 1:
                twin_copy(t).start()

    mine.wait()
    for k in range(DEPTH_CHUNKS):
        relay(k)
        if k > 0:
            project(k - 1)
    project(DEPTH_CHUNKS - 1)

    for t in range(HIDDEN_TILES):
        twin_copy(t).wait_recv()
        total = acc[t] + peer[t]
        gate_sum, up_sum = total[:, :tile], total[:, tile:]
        hid[:, pl.ds(t * tile, tile)] = (gate_sum / (1 + jnp.exp(-gate_sum)) * up_sum).astype(jnp.bfloat16)

    down_copy.wait()

    def ry_copy(n):
        return remote(y_out.at[n], y_in.at[n], rys.at[n], ryr.at[n], across)

    def rz_copy(n, d):
        return remote(z_out.at[n, d], z_in.at[n, zn - d], rzs.at[n, d], rzr.at[n, zn - d], along(d))

    def rb_copy(n, d):
        return remote(b_out.at[n, d], b_in.at[n, zn - d], rbs.at[n, d], rbr.at[n, zn - d], along(d))

    def re_copy(n):
        return remote(e_out.at[n], e_in.at[n], res.at[n], rer.at[n], across)

    for n in range(OUT_CHUNKS):
        products = jnp.dot(hid[...], down[:, pl.ds(n * cols, cols)], preferred_element_type=jnp.float32)
        if n < Z_FIRST:
            blocks = products.reshape(2, zn, rows, cols)
            for d in range(1, zn):
                b_out[n, d] = blocks[:, d].astype(jnp.bfloat16)
                rb_copy(n, d).start()
            own[n, pl.ds(0, 2 * rows)] = blocks[:, 0].reshape(2 * rows, cols)
        else:
            y_out[n] = products[half:].astype(jnp.bfloat16)
            ry_copy(n).start()
            own[n] = products[:half]

    for n in range(Z_FIRST, OUT_CHUNKS):
        ry_copy(n).wait_recv()
        for d in range(zn):
            row = pl.ds(d * rows, rows)
            value = own[n, row] + y_in[n, row].astype(jnp.float32)
            if d == 0:
                own[n, row] = value
            else:
                z_out[n, d] = value.astype(jnp.bfloat16)
                rz_copy(n, d).start()

    for n in range(Z_FIRST):
        value = own[n, pl.ds(0, 2 * rows)]
        for s in range(1, zn):
            rb_copy(n, zn - s).wait_recv()
            value = value + b_in[n, s].astype(jnp.float32).reshape(2 * rows, cols)
        e_out[n] = value[rows:].astype(jnp.bfloat16)
        re_copy(n).start()
        own[n, pl.ds(0, rows)] = value[:rows]

    for n in range(OUT_CHUNKS):
        value = own[n, pl.ds(0, rows)]
        if n < Z_FIRST:
            re_copy(n).wait_recv()
            value = value + e_in[n].astype(jnp.float32)
        else:
            for s in range(1, zn):
                rz_copy(n, zn - s).wait_recv()
                value = value + z_in[n, s].astype(jnp.float32)
        out_ref[:, pl.ds(n * cols, cols)] = value.astype(jnp.bfloat16)

    for k in range(DEPTH_CHUNKS):
        for d in range(zn):
            y_copy(k, d).wait_send()
            if d > 0:
                z_copy(k, d).wait_send()
    for t in range(HIDDEN_TILES):
        twin_copy(t).wait_send()
    for n in range(OUT_CHUNKS):
        if n < Z_FIRST:
            re_copy(n).wait_send()
        else:
            ry_copy(n).wait_send()
        for d in range(1, zn):
            (rb_copy if n < Z_FIRST else rz_copy)(n, d).wait_send()


def solution(mesh):
    wide = mesh.shape["wide"]
    zn = wide // COLUMN

    def body(x, gate, up, down):
        rows, width = x.shape
        units = gate.shape[1]
        half, cols, tile = zn * rows, width // OUT_CHUNKS, units // HIDDEN_TILES
        bf16, f32 = jnp.bfloat16, jnp.float32
        dma = pltpu.SemaphoreType.DMA
        return pl.pallas_call(
            functools.partial(kernel, wide),
            out_shape=jax.ShapeDtypeStruct((rows, width), bf16),
            in_specs=[pl.BlockSpec(memory_space=pltpu.HBM)] * 4,
            out_specs=pl.BlockSpec(memory_space=pltpu.VMEM),
            scratch_shapes=[
                pltpu.VMEM((wide, rows, width), bf16),
                pltpu.VMEM(gate.shape, bf16),
                pltpu.VMEM(up.shape, bf16),
                pltpu.VMEM(down.shape, bf16),
                pltpu.VMEM((HIDDEN_TILES, 2 * half, 2 * tile), f32),
                pltpu.VMEM((HIDDEN_TILES, 2 * half, 2 * tile), f32),
                pltpu.VMEM((2 * half, units), bf16),
                pltpu.VMEM((OUT_CHUNKS, half, cols), f32),
                pltpu.VMEM((OUT_CHUNKS, half, cols), bf16),
                pltpu.VMEM((OUT_CHUNKS, half, cols), bf16),
                pltpu.VMEM((OUT_CHUNKS, zn, rows, cols), bf16),
                pltpu.VMEM((OUT_CHUNKS, zn, rows, cols), bf16),
                pltpu.VMEM((max(Z_FIRST, 1), zn, 2, rows, cols), bf16),
                pltpu.VMEM((max(Z_FIRST, 1), zn, 2, rows, cols), bf16),
                pltpu.VMEM((max(Z_FIRST, 1), rows, cols), bf16),
                pltpu.VMEM((max(Z_FIRST, 1), rows, cols), bf16),
                dma((2, DEPTH_CHUNKS)), dma, dma,
                dma((DEPTH_CHUNKS, zn)), dma((DEPTH_CHUNKS, zn)),
                dma((DEPTH_CHUNKS, zn)), dma((DEPTH_CHUNKS, zn)),
                dma((HIDDEN_TILES,)), dma((HIDDEN_TILES,)),
                dma((OUT_CHUNKS,)), dma((OUT_CHUNKS,)),
                dma((OUT_CHUNKS, zn)), dma((OUT_CHUNKS, zn)),
                dma((max(Z_FIRST, 1), zn)), dma((max(Z_FIRST, 1), zn)),
                dma((max(Z_FIRST, 1),)), dma((max(Z_FIRST, 1),)),
            ],
            compiler_params=pltpu.CompilerParams(
                collective_id=0, has_side_effects=True, vmem_limit_bytes=56 * 1024 * 1024),
        )(x, gate, up, down)

    in_specs = (
        P(("groups", "wide"), "narrow"),
        P("narrow", "wide"),
        P("narrow", "wide"),
        P("wide", "narrow"),
    )
    out_specs = P(("groups", "wide"), "narrow")
    return jax.shard_map(body, mesh=mesh, in_specs=in_specs, out_specs=out_specs, check_vma=False)
```

```python
import functools

import jax
import jax.numpy as jnp
from jax import lax
from jax.experimental import pallas as pl
from jax.experimental.pallas import tpu as pltpu
from jax.sharding import PartitionSpec as P

MESH = pl.DeviceIdType.MESH
COLUMN = 2
DEPTH_PARTS = (1, 2, 1)
DEPTH_CHUNKS = len(DEPTH_PARTS)
HIDDEN_TILES = 1
OUT_CHUNKS = 8
Z_FIRST = 2


def kernel(wide, x_hbm, gate_hbm, up_hbm, down_hbm, out_ref,
           xg, gate, up, down, acc, peer, hid, own, y_out, y_in, z_out, z_in, b_out, b_in, e_out, e_in,
           w_sem, d_sem, x_sem, zs, zr, ys, yr, ns, nr, rys, ryr, rzs, rzr,
           rbs, rbr, res, rer):
    zn = wide // COLUMN
    rows, width = x_hbm.shape
    half = zn * rows
    units = gate_hbm.shape[1]
    unit = width // sum(DEPTH_PARTS)
    tile = units // HIDDEN_TILES
    cols = width // OUT_CHUNKS

    me = lax.axis_index("wide")
    z, y = me // COLUMN, lax.rem(me, COLUMN)
    core = lax.axis_index("narrow")
    across = {"wide": z * COLUMN + (1 - y)}
    twin = {"narrow": 1 - core}

    def along(d):
        return {"wide": lax.rem(z + d, zn) * COLUMN + y}

    def span(k):
        return pl.ds(sum(DEPTH_PARTS[:k]) * unit, DEPTH_PARTS[k] * unit)

    def local(k):
        part = span(k)
        return [
            pltpu.make_async_copy(gate_hbm.at[part], gate.at[part], w_sem.at[0, k]),
            pltpu.make_async_copy(up_hbm.at[part], up.at[part], w_sem.at[1, k]),
        ]

    def remote(src, dst, send, recv, to):
        return pltpu.make_async_remote_copy(
            src_ref=src, dst_ref=dst, send_sem=send, recv_sem=recv, device_id=to, device_id_type=MESH)

    barrier = pltpu.get_barrier_semaphore()
    for d in range(1, zn):
        pl.semaphore_signal(barrier, inc=1, device_id=along(d), device_id_type=MESH)
    pl.semaphore_signal(barrier, inc=1, device_id=across, device_id_type=MESH)
    pl.semaphore_signal(barrier, inc=1, device_id=twin, device_id_type=MESH)
    mine = pltpu.make_async_copy(x_hbm, xg.at[0], x_sem)
    mine.start()
    for k in range(DEPTH_CHUNKS):
        for copy in local(k):
            copy.start()
    down_copy = pltpu.make_async_copy(down_hbm, down, d_sem)
    down_copy.start()
    pl.semaphore_wait(barrier, zn + 1)

    def z_copy(k, d):
        part = span(k)
        return remote(x_hbm.at[:, part], xg.at[zn - d, :, part], zs.at[k, d], zr.at[k, zn - d], along(d))

    def y_copy(k, s):
        part = span(k)
        src = x_hbm.at[:, part] if s == 0 else xg.at[s, :, part]
        return remote(src, xg.at[zn + s, :, part], ys.at[k, s], yr.at[k, s], across)

    for k in range(DEPTH_CHUNKS):
        y_copy(k, 0).start()
        for d in range(1, zn):
            z_copy(k, d).start()

    def relay(k):
        for s in sorted(range(1, zn), key=lambda s: min(s, zn - s)):
            z_copy(k, zn - s).wait_recv()
            y_copy(k, s).start()

    def twin_copy(t):
        return remote(acc.at[t], peer.at[t], ns.at[t], nr.at[t], twin)

    def project(k):
        for s in range(zn):
            y_copy(k, s).wait_recv()
        for copy in local(k):
            copy.wait()
        part = span(k)
        x = xg[:, :, part].reshape(2 * half, DEPTH_PARTS[k] * unit)
        for t in range(HIDDEN_TILES):
            mid = pl.ds(t * tile, tile)
            for i, weight in enumerate((gate, up)):
                value = jnp.dot(x, weight[part, mid], preferred_element_type=jnp.float32)
                place = pl.ds(i * tile, tile)
                if k == 0:
                    acc[t, :, place] = value
                else:
                    acc[t, :, place] += value
            if k == DEPTH_CHUNKS - 1:
                twin_copy(t).start()

    mine.wait()
    for k in range(DEPTH_CHUNKS):
        relay(k)
        if k > 0:
            project(k - 1)
    project(DEPTH_CHUNKS - 1)

    for t in range(HIDDEN_TILES):
        twin_copy(t).wait_recv()
        total = acc[t] + peer[t]
        gate_sum, up_sum = total[:, :tile], total[:, tile:]
        hid[:, pl.ds(t * tile, tile)] = (gate_sum / (1 + jnp.exp(-gate_sum)) * up_sum).astype(jnp.bfloat16)

    down_copy.wait()

    def ry_copy(n):
        return remote(y_out.at[n], y_in.at[n], rys.at[n], ryr.at[n], across)

    def rz_copy(n, d):
        return remote(z_out.at[n, d], z_in.at[n, zn - d], rzs.at[n, d], rzr.at[n, zn - d], along(d))

    def rb_copy(n, d):
        return remote(b_out.at[n, d], b_in.at[n, zn - d], rbs.at[n, d], rbr.at[n, zn - d], along(d))

    def re_copy(n):
        return remote(e_out.at[n], e_in.at[n], res.at[n], rer.at[n], across)

    for n in range(OUT_CHUNKS):
        products = jnp.dot(hid[...], down[:, pl.ds(n * cols, cols)], preferred_element_type=jnp.float32)
        if n < Z_FIRST:
            blocks = products.reshape(2, zn, rows, cols)
            for d in range(1, zn):
                b_out[n, d] = blocks[:, d].astype(jnp.bfloat16)
                rb_copy(n, d).start()
            own[n, pl.ds(0, 2 * rows)] = blocks[:, 0].reshape(2 * rows, cols)
        else:
            y_out[n] = products[half:].astype(jnp.bfloat16)
            ry_copy(n).start()
            own[n] = products[:half]

    for k in range(DEPTH_CHUNKS):
        for d in range(zn):
            y_copy(k, d).wait_send()
            if d > 0:
                z_copy(k, d).wait_send()
    for t in range(HIDDEN_TILES):
        twin_copy(t).wait_send()

    for n in range(Z_FIRST, OUT_CHUNKS):
        ry_copy(n).wait_recv()
        for d in sorted(range(zn), key=lambda d: -min(d, zn - d)):
            row = pl.ds(d * rows, rows)
            value = own[n, row] + y_in[n, row].astype(jnp.float32)
            if d == 0:
                own[n, row] = value
            else:
                z_out[n, d] = value.astype(jnp.bfloat16)
                rz_copy(n, d).start()

    for n in range(Z_FIRST):
        value = own[n, pl.ds(0, 2 * rows)]
        for s in range(1, zn):
            rb_copy(n, zn - s).wait_recv()
            value = value + b_in[n, s].astype(jnp.float32).reshape(2 * rows, cols)
        e_out[n] = value[rows:].astype(jnp.bfloat16)
        re_copy(n).start()
        own[n, pl.ds(0, rows)] = value[:rows]

    for n in range(OUT_CHUNKS):
        value = own[n, pl.ds(0, rows)]
        if n < Z_FIRST:
            re_copy(n).wait_recv()
            value = value + e_in[n].astype(jnp.float32)
        else:
            for s in range(1, zn):
                rz_copy(n, zn - s).wait_recv()
                value = value + z_in[n, s].astype(jnp.float32)
        out_ref[:, pl.ds(n * cols, cols)] = value.astype(jnp.bfloat16)

    for n in range(OUT_CHUNKS):
        if n < Z_FIRST:
            re_copy(n).wait_send()
        else:
            ry_copy(n).wait_send()
        for d in range(1, zn):
            (rb_copy if n < Z_FIRST else rz_copy)(n, d).wait_send()


def solution(mesh):
    wide = mesh.shape["wide"]
    zn = wide // COLUMN

    def body(x, gate, up, down):
        rows, width = x.shape
        units = gate.shape[1]
        half, cols, tile = zn * rows, width // OUT_CHUNKS, units // HIDDEN_TILES
        bf16, f32 = jnp.bfloat16, jnp.float32
        dma = pltpu.SemaphoreType.DMA
        return pl.pallas_call(
            functools.partial(kernel, wide),
            out_shape=jax.ShapeDtypeStruct((rows, width), bf16),
            in_specs=[pl.BlockSpec(memory_space=pltpu.HBM)] * 4,
            out_specs=pl.BlockSpec(memory_space=pltpu.VMEM),
            scratch_shapes=[
                pltpu.VMEM((wide, rows, width), bf16),
                pltpu.VMEM(gate.shape, bf16),
                pltpu.VMEM(up.shape, bf16),
                pltpu.VMEM(down.shape, bf16),
                pltpu.VMEM((HIDDEN_TILES, 2 * half, 2 * tile), f32),
                pltpu.VMEM((HIDDEN_TILES, 2 * half, 2 * tile), f32),
                pltpu.VMEM((2 * half, units), bf16),
                pltpu.VMEM((OUT_CHUNKS, half, cols), f32),
                pltpu.VMEM((OUT_CHUNKS, half, cols), bf16),
                pltpu.VMEM((OUT_CHUNKS, half, cols), bf16),
                pltpu.VMEM((OUT_CHUNKS, zn, rows, cols), bf16),
                pltpu.VMEM((OUT_CHUNKS, zn, rows, cols), bf16),
                pltpu.VMEM((max(Z_FIRST, 1), zn, 2, rows, cols), bf16),
                pltpu.VMEM((max(Z_FIRST, 1), zn, 2, rows, cols), bf16),
                pltpu.VMEM((max(Z_FIRST, 1), rows, cols), bf16),
                pltpu.VMEM((max(Z_FIRST, 1), rows, cols), bf16),
                dma((2, DEPTH_CHUNKS)), dma, dma,
                dma((DEPTH_CHUNKS, zn)), dma((DEPTH_CHUNKS, zn)),
                dma((DEPTH_CHUNKS, zn)), dma((DEPTH_CHUNKS, zn)),
                dma((HIDDEN_TILES,)), dma((HIDDEN_TILES,)),
                dma((OUT_CHUNKS,)), dma((OUT_CHUNKS,)),
                dma((OUT_CHUNKS, zn)), dma((OUT_CHUNKS, zn)),
                dma((max(Z_FIRST, 1), zn)), dma((max(Z_FIRST, 1), zn)),
                dma((max(Z_FIRST, 1),)), dma((max(Z_FIRST, 1),)),
            ],
            compiler_params=pltpu.CompilerParams(
                collective_id=0, has_side_effects=True, vmem_limit_bytes=56 * 1024 * 1024),
        )(x, gate, up, down)

    in_specs = (
        P(("groups", "wide"), "narrow"),
        P("narrow", "wide"),
        P("narrow", "wide"),
        P("wide", "narrow"),
    )
    out_specs = P(("groups", "wide"), "narrow")
    return jax.shard_map(body, mesh=mesh, in_specs=in_specs, out_specs=out_specs, check_vma=False)
```
